256 devices in a mesh: rep: 8 (over x_lo, y), blk: 32 (over z, x_hi, core).
Axes of the slice: x: 4 (x_hi: 2, x_lo: 2; x = x_hi * 2 + x_lo), y: 4, z: 8, core: 2. Of those that a mesh axis runs over, the one named last changes fastest.
Arguments:
- features: bfloat16 [32, 4096, 128], P('blk', 'rep'), may hold values from -6 to 6
- weight: bfloat16 [128, 256], replicated, may hold values from -0.5 to 0.5
- cotangent: bfloat16 [32, 4096, 256], P('blk', 'rep'), may hold values from -6 to 6
- self_weight: float32 [32, 4096], P('blk', 'rep'), may hold values from 0.3 to 1.5
- block_rows: int32 [8, 32, 384], P('rep', 'blk'), may hold values from 0 to 127, as said below
- block_cols: int32 [8, 32, 384], P('rep', 'blk'), may hold values from 0 to 31, as said below
- block_counts: int32 [8, 32], P('rep', 'blk'), may hold values from 1 to 384, as said below
- block_values: bfloat16 [8, 32, 384, 128, 128], P('rep', 'blk'), as said below
Outputs:
- activated: bfloat16 [32, 4096, 256], P('blk', 'rep')
- feature_grad: bfloat16 [32, 4096, 128], P('blk', 'rep')
- weight_grad: float32 [128, 256], P('rep')
The draws below stay inside these ranges and needn't reach their ends.
Inputs may be any that keep to these rules, and one draw needn't show every extreme that they name: `block_counts`: one device of every draw has all 384 slots live. `block_rows`: the live slots of one device name distinct (row tile, column tile) pairs; slots past the count hold 0. `block_cols`: slots past the count hold 0. `block_values`: slots at or past a device's count hold zeros.
All inputs are finite; a program needn't handle non-finite values.
Results may differ from the reference program's by a relative error of at most 0.024.
Values may be sent and summed in bfloat16 or wider, within the bound.
No kernel may reach another device: no remote copies, remote signals or barrier semaphores. Data moves between devices by JAX's collectives and lax.ppermute only.
A program may use at most 128 MiB of HBM per device.

```python
import math
import jax
import jax.numpy as jnp
from jax import lax

F = 128
H = 256
BS = 128
ROWS_DEV = 512
CAP = 384
PANEL_ROWS = 4096
N_REP = 8
N_BLK = 32


def block_layout(key):
    row_tiles = N_BLK * ROWS_DEV // BS
    col_tiles = N_REP * ROWS_DEV // BS
    device_total = N_REP * N_BLK
    spread = jax.random.randint(jax.random.fold_in(key, 11), (device_total,), CAP // 6, CAP // 2 + 1)
    busiest = jax.random.randint(jax.random.fold_in(key, 12), (), 0, device_total)
    count_list = jnp.where(jnp.arange(device_total) == busiest, CAP, spread).astype(jnp.int32)
    key_list = jax.random.split(jax.random.fold_in(key, 13), device_total)
    pair_ids = jax.vmap(lambda one_key: jax.random.permutation(one_key, row_tiles * col_tiles)[:CAP])(key_list)
    is_live = jnp.arange(CAP)[None, :] < count_list[:, None]
    tile_rows = jnp.where(is_live, pair_ids // col_tiles, 0).astype(jnp.int32)
    tile_cols = jnp.where(is_live, pair_ids % col_tiles, 0).astype(jnp.int32)
    return (count_list, tile_rows, tile_cols)


def draw_block_counts(key, part):
    shared = block_layout(key)
    return shared[0].reshape(N_REP, N_BLK)


def draw_block_rows(key, part):
    shared = block_layout(key)
    return shared[1].reshape(N_REP, N_BLK, CAP)


def draw_block_cols(key, part):
    shared = block_layout(key)
    return shared[2].reshape(N_REP, N_BLK, CAP)


def draw_block_values(key, part):
    shared = block_layout(key)
    key = jax.random.fold_in(key, 4)
    scale = (6.0 * ROWS_DEV / (CAP * BS * BS)) ** 0.5
    live_rows = (jnp.arange(CAP)[None, :] < shared[0][:, None]).astype(jnp.float32)

    def one_device(inputs):
        index, live_row = inputs
        dev_key = jax.random.fold_in(key, index)
        keep = jax.random.bernoulli(jax.random.fold_in(dev_key, 1), 0.5, (CAP, BS, BS)).astype(jnp.float32)
        entries = jax.random.normal(jax.random.fold_in(dev_key, 2), (CAP, BS, BS), jnp.float32)
        return (entries * keep * scale * live_row[:, None, None]).astype(jnp.bfloat16)
    tiles_all = lax.map(one_device, (jnp.arange(N_REP * N_BLK, dtype=jnp.int32), live_rows))
    return tiles_all.reshape(N_REP, N_BLK, CAP, BS, BS)


def block_levels(key, dims, shards, least, top_value):
    factor_of = 1.0
    for axis_at, parts in shards:
        heights = jax.random.uniform(jax.random.fold_in(jax.random.fold_in(key, 6), axis_at), (parts,), jnp.float32, least / len(shards), top_value / len(shards))
        factor_of = factor_of * jnp.repeat(jnp.exp(heights), dims[axis_at] // parts).reshape((-1,) + (1,) * (len(dims) - 1 - axis_at))
    return factor_of


def scatter_about(key, shape, width, limit, pieces=(), held_as=jnp.bfloat16):
    gain = block_levels(key, shape, pieces, -0.22, 0.18) if pieces else 1.0
    array = jax.random.normal(key, shape, jnp.float32) * width * gain
    return jnp.minimum(jnp.maximum(array, -limit), limit).astype(held_as)


def setup_inputs(seed: int = 0) -> dict:
    key_of = jax.random.split(jax.random.key(seed), 9)
    return {
        "features": scatter_about(key_of[0], (N_BLK, PANEL_ROWS, F), 1.0, 6.0, ((0, 32), (1, 8))),
        "weight": scatter_about(key_of[1], (F, H), F ** -0.5, 0.5),
        "cotangent": scatter_about(key_of[2], (N_BLK, PANEL_ROWS, H), 1.0, 6.0, ((0, 32), (1, 8))),
        "self_weight": jnp.clip(jnp.exp(math.log(1.5) - 1.60943787 * jax.random.uniform(key_of[3], (N_BLK, PANEL_ROWS), jnp.float32) ** block_levels(key_of[3], (N_BLK, PANEL_ROWS), ((0, 32), (1, 8)), -0.2, 0.2)), 0.3, 1.5),
        "block_rows": draw_block_rows(jax.random.fold_in(key_of[8], 71), 0),
        "block_cols": draw_block_cols(jax.random.fold_in(key_of[8], 71), 0),
        "block_counts": draw_block_counts(jax.random.fold_in(key_of[8], 71), 0),
        "block_values": draw_block_values(jax.random.fold_in(key_of[8], 71), 0),
    }


def silu_slope(pre_act):
    sigma = jax.nn.sigmoid(pre_act)
    return sigma * (1.0 + pre_act * (1.0 - sigma))

def reference(features, weight, cotangent, self_weight, block_rows, block_cols, block_counts, block_values):
    panel_rows = N_REP * ROWS_DEV
    row_tiles = N_BLK * ROWS_DEV // BS
    col_tiles = panel_rows // BS
    slot_ids = jnp.arange(CAP, dtype=jnp.int32)
    device_ids = jnp.arange(N_REP * N_BLK, dtype=jnp.int32)

    def device_tiles(index):
        rep_at = index // N_BLK
        blk_at = index % N_BLK
        tile_data = block_values[rep_at, blk_at].astype(jnp.float32)
        is_live = (slot_ids < block_counts[rep_at, blk_at]).astype(jnp.float32)
        return (rep_at, blk_at, tile_data * is_live[:, None, None], block_rows[rep_at, blk_at], block_cols[rep_at, blk_at])

    def forward_step(summed, index):
        rep_at, blk_at, tile_data, rows_here, cols_here = device_tiles(index)
        panel = lax.dynamic_index_in_dim(features, blk_at, 0, keepdims=False).astype(jnp.float32)
        panel = panel.reshape(col_tiles, BS, F)
        products = jnp.einsum('sij,sjf->sif', tile_data, panel[cols_here])
        term = jnp.zeros((row_tiles, BS, F), jnp.float32).at[rows_here].add(products)
        term = lax.optimization_barrier(term.astype(jnp.bfloat16)).astype(jnp.float32)
        term = term.reshape(N_BLK, 1, ROWS_DEV, F)
        current = lax.dynamic_slice_in_dim(summed, rep_at, 1, 1)
        return (lax.dynamic_update_slice_in_dim(summed, current + term, rep_at, 1), None)
    summed = lax.scan(forward_step, jnp.zeros((N_BLK, N_REP, ROWS_DEV, F), jnp.float32), device_ids)[0]
    own_rows = features.astype(jnp.float32)
    aggregated = (summed.reshape(N_BLK, panel_rows, F) + self_weight[:, :, None] * own_rows).astype(jnp.bfloat16)
    flat_agg = aggregated.reshape(N_BLK * panel_rows, F)
    pre_act = jnp.dot(flat_agg, weight, preferred_element_type=jnp.float32)
    activated = jax.nn.silu(pre_act).astype(jnp.bfloat16)
    slope = (cotangent.reshape(N_BLK * panel_rows, H).astype(jnp.float32) * silu_slope(pre_act)).astype(jnp.bfloat16)
    weight_grad = jnp.dot(flat_agg.T, slope, preferred_element_type=jnp.float32) / math.sqrt(N_BLK * panel_rows)
    row_grad = jnp.dot(slope, weight.T, preferred_element_type=jnp.float32).astype(jnp.bfloat16)
    grid_grad = row_grad.reshape(N_BLK, N_REP, ROWS_DEV, F)

    def backward_step(columns, index):
        rep_at, blk_at, tile_data, rows_here, cols_here = device_tiles(index)
        source = lax.dynamic_index_in_dim(grid_grad, rep_at, 1, keepdims=False).astype(jnp.float32)
        source = source.reshape(row_tiles, BS, F)
        products = jnp.einsum('sji,sjf->sif', tile_data, source[rows_here])
        term = jnp.zeros((col_tiles, BS, F), jnp.float32).at[cols_here].add(products)
        term = term.reshape(1, panel_rows, F)
        current = lax.dynamic_slice_in_dim(columns, blk_at, 1, 0)
        return (lax.dynamic_update_slice_in_dim(columns, current + term, blk_at, 0), None)
    columns = lax.scan(backward_step, jnp.zeros((N_BLK, panel_rows, F), jnp.float32), device_ids)[0]
    own_grad = self_weight[:, :, None] * row_grad.reshape(N_BLK, panel_rows, F).astype(jnp.float32)
    feature_grad = (columns + own_grad).astype(jnp.bfloat16)
    return (activated.reshape(N_BLK, panel_rows, H), feature_grad, weight_grad)
```

```python
import math

import jax
import jax.numpy as jnp
from jax import lax
from jax.experimental import pallas as pl
from jax.experimental.pallas import tpu as pltpu
from jax.sharding import Mesh
from jax.sharding import PartitionSpec as P

AXES = ("xl", "y", "z", "xh", "c")
SIZES = (2, 4, 8, 2, 2)
REP = ("xl", "y")
BLK = ("z", "xh", "c")
NZ = 8
BS = 128
GROUP = 32
BUFFERS = 4


def _pairs(move):
    pairs = []
    for xl in range(2):
        for y in range(4):
            for z in range(8):
                for xh in range(2):
                    for c in range(2):
                        src = (xl, y, z, xh, c)
                        flat = []
                        for at in (src, move(*src)):
                            index = 0
                            for size, value in zip(SIZES, at):
                                index = index * size + value
                            flat.append(index)
                        pairs.append(tuple(flat))
    return pairs


def z_shift(k):
    return _pairs(lambda xl, y, z, xh, c: (xl, y, (z + k) % 8, xh, c))


def z_flip(k):
    return _pairs(lambda xl, y, z, xh, c: (xl, y, z ^ k, xh, c))


CORE_SWAP = _pairs(lambda xl, y, z, xh, c: (xl, y, z, xh, 1 - c))
X_SWAP = _pairs(lambda xl, y, z, xh, c: (xl, y, z, 1 - xh, c))


def send(value, pairs):
    return lax.ppermute(value, AXES, pairs)


def stream_tiles(count, tiles_ref, buf, sems, use):
    groups = (count + GROUP - 1) // GROUP

    def copy(group, slot):
        return pltpu.make_async_copy(
            tiles_ref.at[pl.ds(group * GROUP, GROUP)], buf.at[slot], sems.at[slot]
        )

    for first in range(BUFFERS - 1):

        @pl.when(first < groups)
        def _():
            copy(first, first).start()

    def one_group(group, carry):
        slot = lax.rem(group, BUFFERS)
        copy(group, slot).wait()

        @pl.when(group + BUFFERS - 1 < groups)
        def _():
            copy(group + BUFFERS - 1, lax.rem(group + BUFFERS - 1, BUFFERS)).start()

        for j in range(GROUP):
            use(group * GROUP + j, slot, j)
        return carry

    return lambda: lax.fori_loop(0, groups, one_group, 0)


def forward_kernel(
    land_ref, cols_ref, count_ref, panel_ref, tiles_ref, keep_ref, away_ref, acc, buf, sems
):
    def use(s, slot, j):
        acc[land_ref[s]] += jnp.dot(
            buf[slot, j], panel_ref[cols_ref[s]], preferred_element_type=jnp.float32
        )

    run = stream_tiles(count_ref[0], tiles_ref, buf, sems, use)
    acc[...] = jnp.zeros_like(acc)
    run()
    half = acc.shape[0] // 2
    keep_ref[...] = acc[:half].astype(jnp.bfloat16)
    away_ref[...] = acc[half:].astype(jnp.bfloat16)


def forward_products(land, cols, count, panel, tiles):
    smem = pl.BlockSpec(memory_space=pltpu.SMEM)
    vmem = pl.BlockSpec(memory_space=pltpu.VMEM)
    half = jax.ShapeDtypeStruct((64, BS, BS), jnp.bfloat16)
    return pl.pallas_call(
        forward_kernel,
        out_shape=(half, half),
        in_specs=[smem, smem, smem, vmem, pl.BlockSpec(memory_space=pl.ANY)],
        out_specs=(vmem, vmem),
        scratch_shapes=[
            pltpu.VMEM((128, BS, BS), jnp.float32),
            pltpu.VMEM((BUFFERS, GROUP, BS, BS), jnp.bfloat16),
            pltpu.SemaphoreType.DMA((BUFFERS,)),
        ],
        compiler_params=pltpu.CompilerParams(vmem_limit_bytes=40 << 20),
        cost_estimate=pl.CostEstimate(
            flops=384 * 2 * BS**3, bytes_accessed=18 << 20, transcendentals=0
        ),
        name="forward_products",
    )(land, cols, count, panel, tiles)


def backward_kernel(
    land_ref, cols_ref, count_ref, *refs
):
    piece_refs = refs[:-6]
    tiles_ref, out_ref, acc, buf, grads, sems = refs[-6:]

    def use(s, slot, j):
        acc[cols_ref[s]] += lax.dot_general(
            buf[slot, j],
            grads[land_ref[s]],
            (((0,), (0,)), ((), ())),
            preferred_element_type=jnp.float32,
        )

    copies = []
    at = 0
    for i, ref in enumerate(piece_refs):
        size = ref.shape[0]
        copies.append(
            pltpu.make_async_copy(ref, grads.at[pl.ds(at, size)], sems.at[BUFFERS + i])
        )
        at += size
    for one in copies:
        one.start()
    run = stream_tiles(count_ref[0], tiles_ref, buf, sems, use)
    acc[...] = jnp.zeros_like(acc)
    for one in copies:
        one.wait()
    run()
    out_ref[...] = acc[...].astype(jnp.bfloat16)


def backward_products(land, cols, count, pieces, tiles):
    smem = pl.BlockSpec(memory_space=pltpu.SMEM)
    vmem = pl.BlockSpec(memory_space=pltpu.VMEM)
    hbm = pl.BlockSpec(memory_space=pl.ANY)
    return pl.pallas_call(
        backward_kernel,
        out_shape=jax.ShapeDtypeStruct((32, BS, BS), jnp.bfloat16),
        in_specs=[smem, smem, smem] + [hbm] * (len(pieces) + 1),
        out_specs=vmem,
        scratch_shapes=[
            pltpu.VMEM((32, BS, BS), jnp.float32),
            pltpu.VMEM((BUFFERS, GROUP, BS, BS), jnp.bfloat16),
            pltpu.VMEM((128, BS, BS), jnp.bfloat16),
            pltpu.SemaphoreType.DMA((BUFFERS + len(pieces),)),
        ],
        compiler_params=pltpu.CompilerParams(vmem_limit_bytes=40 << 20),
        cost_estimate=pl.CostEstimate(
            flops=384 * 2 * BS**3, bytes_accessed=18 << 20, transcendentals=0
        ),
        name="backward_products",
    )(land, cols, count, *pieces, tiles)


def add_pair(a, b):
    return (a.astype(jnp.float32) + b.astype(jnp.float32)).astype(jnp.bfloat16)


def dense(summed, scale, features, weight, cotangent):
    aggregated = (summed + scale * features.astype(jnp.float32)).astype(jnp.bfloat16)
    pre_act = jnp.dot(aggregated, weight, preferred_element_type=jnp.float32)
    sigma = jax.nn.sigmoid(pre_act)
    activated = (pre_act * sigma).astype(jnp.bfloat16)
    slope = (
        cotangent.astype(jnp.float32) * (sigma * (1.0 + pre_act * (1.0 - sigma)))
    ).astype(jnp.bfloat16)
    weight_part = lax.dot_general(
        aggregated, slope, (((0,), (0,)), ((), ())), preferred_element_type=jnp.float32
    )
    row_grad = lax.dot_general(
        slope, weight, (((1,), (1,)), ((), ())), preferred_element_type=jnp.float32
    ).astype(jnp.bfloat16)
    return activated, weight_part, row_grad


def on_device(
    features, weight, cotangent, self_weight, block_rows, block_cols, block_counts, block_values
):
    tiles = block_values[0, 0]
    rows = block_rows[0, 0]
    cols = block_cols[0, 0]
    count = block_counts[0]
    z = lax.axis_index("z")
    xh = lax.axis_index("xh")
    c = lax.axis_index("c")
    panel_at = rows // 4
    q = rows % 4
    half, low = q // 2, q % 2
    row_z, row_x, row_c = panel_at // 4, (panel_at // 2) % 2, panel_at % 2
    rel_c, rel_x = row_c ^ c, row_x ^ xh
    rel_out = (row_z - z) % NZ
    rel_in = (z - row_z) % NZ
    land_fwd = (((rel_c * 2 + half) * 2 + rel_x) * NZ + rel_out) * 2 + low
    land_bwd = (
        rel_c * 64
        + half * 32
        + jnp.where(half == 0, rel_in * 4 + rel_x * 2, rel_x * 16 + rel_in * 2)
        + low
    )

    panel = lax.all_to_all(jnp.broadcast_to(features, (8, 512, BS)), REP, 0, 0)
    keep, away = forward_products(land_fwd, cols, count, panel.reshape(32, BS, BS), tiles)
    summed = add_pair(keep, send(away, CORE_SWAP)).reshape(2, 2, NZ, 256, BS)

    first = add_pair(summed[0, 0], send(summed[0, 1], X_SWAP))
    total_a = first[0].astype(jnp.float32)
    for k in range(1, NZ):
        total_a = total_a + send(first[k], z_shift(k)).astype(jnp.float32)
    second = summed[1]
    total_b = second[:, 0].astype(jnp.float32)
    for k in range(1, NZ):
        total_b = total_b + send(second[:, k], z_shift(k)).astype(jnp.float32)
    total_b = total_b[0] + send(total_b[1].astype(jnp.bfloat16), X_SWAP).astype(jnp.float32)

    scale = self_weight[0][:, None]
    act_a, weight_a, grad_a = dense(
        total_a, scale[:256], features[0, :256], weight, cotangent[0, :256]
    )
    act_b, weight_b, grad_b = dense(
        total_b, scale[256:], features[0, 256:], weight, cotangent[0, 256:]
    )
    activated = jnp.concatenate([act_a, act_b], 0)[None]

    pair = jnp.stack([grad_a, send(grad_a, X_SWAP)])
    got_a = jnp.stack([pair] + [send(pair, z_shift(k)) for k in range(1, NZ)])
    got_b = jnp.stack([grad_b] + [send(grad_b, z_shift(k)) for k in range(1, NZ)])
    got_bx = send(got_b, X_SWAP)
    pieces = [got_a, got_b, got_bx]
    pieces = pieces + [send(piece, CORE_SWAP) for piece in pieces]
    pieces = [piece.reshape(-1, BS, BS) for piece in pieces]
    columns = backward_products(land_bwd, cols, count, pieces, tiles)
    parts = lax.all_to_all(columns.reshape(8, 512, BS), REP, 0, 0)
    row_grad = jnp.concatenate([grad_a, grad_b], 0)
    feature_grad = (
        jnp.sum(parts.astype(jnp.float32), 0) + scale * row_grad.astype(jnp.float32)
    ).astype(jnp.bfloat16)[None]

    node_total = 32 * 8 * 512
    weight_sum = (weight_a + weight_b) * (1.0 / math.sqrt(node_total))
    weight_sum = jnp.sum(lax.all_to_all(weight_sum.reshape(8, 16, 256), REP, 0, 0), 0)
    for move in (CORE_SWAP, X_SWAP, z_flip(1), z_flip(2), z_flip(4)):
        weight_sum = weight_sum + send(weight_sum, move)
    return activated, feature_grad, weight_sum


def solution(mesh):
    fine = Mesh(mesh.devices.reshape(SIZES), AXES)
    placed = (
        P(BLK, REP, None),
        P(),
        P(BLK, REP, None),
        P(BLK, REP),
        P(REP, BLK, None),
        P(REP, BLK, None),
        P(REP, BLK),
        P(REP, BLK, None, None, None),
    )
    return jax.shard_map(
        on_device,
        mesh=fine,
        in_specs=placed,
        out_specs=(P(BLK, REP, None), P(BLK, REP, None), P(REP, None)),
        check_vma=False,
    )
```

```python
import math

import jax
import jax.numpy as jnp
from jax import lax
from jax.experimental import pallas as pl
from jax.experimental.pallas import tpu as pltpu
from jax.sharding import Mesh
from jax.sharding import PartitionSpec as P

AXES = ("xl", "y", "z", "xh", "c")
SIZES = (2, 4, 8, 2, 2)
REP = ("xl", "y")
BLK = ("z", "xh", "c")
NZ = 8
BS = 128
GROUP = 32
BUFFERS = 4


def _pairs(move):
    pairs = []
    for xl in range(2):
        for y in range(4):
            for z in range(8):
                for xh in range(2):
                    for c in range(2):
                        src = (xl, y, z, xh, c)
                        flat = []
                        for at in (src, move(*src)):
                            index = 0
                            for size, value in zip(SIZES, at):
                                index = index * size + value
                            flat.append(index)
                        pairs.append(tuple(flat))
    return pairs


def z_flip(k):
    return _pairs(lambda xl, y, z, xh, c: (xl, y, z ^ k, xh, c))


Z_RING = _pairs(lambda xl, y, z, xh, c: (xl, y, (z + 1 - 2 * c) % 8, xh, c))
REP_SWAPS = (
    _pairs(lambda xl, y, z, xh, c: (1 - xl, y, z, xh, c)),
    _pairs(lambda xl, y, z, xh, c: (xl, y ^ 2, z, xh, c)),
    _pairs(lambda xl, y, z, xh, c: (xl, y ^ 1, z, xh, c)),
)
CORE_SWAP = _pairs(lambda xl, y, z, xh, c: (xl, y, z, xh, 1 - c))
X_SWAP = _pairs(lambda xl, y, z, xh, c: (xl, y, z, 1 - xh, c))


def send(value, pairs):
    return lax.ppermute(value, AXES, pairs)


def stream_tiles(count, tiles_ref, buf, sems, use):
    groups = (count + GROUP - 1) // GROUP

    def copy(group, slot):
        return pltpu.make_async_copy(
            tiles_ref.at[pl.ds(group * GROUP, GROUP)], buf.at[slot], sems.at[slot]
        )

    for first in range(BUFFERS - 1):

        @pl.when(first < groups)
        def _():
            copy(first, first).start()

    def one_group(group, carry):
        slot = lax.rem(group, BUFFERS)
        copy(group, slot).wait()

        @pl.when(group + BUFFERS - 1 < groups)
        def _():
            copy(group + BUFFERS - 1, lax.rem(group + BUFFERS - 1, BUFFERS)).start()

        for j in range(GROUP):
            use(group * GROUP + j, slot, j)
        return carry

    return lambda: lax.fori_loop(0, groups, one_group, 0)


def forward_kernel(
    land_ref, cols_ref, count_ref, panel_ref, tiles_ref, keep_ref, away_far_ref, away_near_ref, acc, buf, sems
):
    def use(s, slot, j):
        acc[land_ref[s]] += jnp.dot(
            buf[slot, j], panel_ref[cols_ref[s]], preferred_element_type=jnp.float32
        )

    run = stream_tiles(count_ref[0], tiles_ref, buf, sems, use)
    acc[...] = jnp.zeros_like(acc)
    run()
    away_far_ref[...] = acc[96:].astype(jnp.bfloat16)
    away_near_ref[...] = acc[64:96].astype(jnp.bfloat16)
    keep_ref[...] = acc[:64].astype(jnp.bfloat16)


def forward_products(land, cols, count, panel, tiles):
    smem = pl.BlockSpec(memory_space=pltpu.SMEM)
    vmem = pl.BlockSpec(memory_space=pltpu.VMEM)
    kept = jax.ShapeDtypeStruct((64, BS, BS), jnp.bfloat16)
    away = jax.ShapeDtypeStruct((32, BS, BS), jnp.bfloat16)
    return pl.pallas_call(
        forward_kernel,
        out_shape=(kept, away, away),
        in_specs=[smem, smem, smem, vmem, pl.BlockSpec(memory_space=pl.ANY)],
        out_specs=(vmem, vmem, vmem),
        scratch_shapes=[
            pltpu.VMEM((128, BS, BS), jnp.float32),
            pltpu.VMEM((BUFFERS, GROUP, BS, BS), jnp.bfloat16),
            pltpu.SemaphoreType.DMA((BUFFERS,)),
        ],
        compiler_params=pltpu.CompilerParams(vmem_limit_bytes=40 << 20),
        cost_estimate=pl.CostEstimate(
            flops=384 * 2 * BS**3, bytes_accessed=18 << 20, transcendentals=0
        ),
        name="forward_products",
    )(land, cols, count, panel, tiles)


def piece_plan(refs):
    near, far, cores = refs[:5], refs[5:10], refs[10:]
    plan = []
    at = 0
    for side, ring in enumerate((near, far)):
        for ref in ring:
            plan.append((ref, 0, at, ref.shape[0]))
            at += ref.shape[0]
        for ref in cores:
            size = ref.shape[0] // 2
            plan.append((ref, side * size, at, size))
            at += size
    return plan


def backward_kernel(land_ref, cols_ref, count_ref, *refs):
    piece_refs = refs[:-6]
    tiles_ref, out_ref, acc, buf, grads, sems = refs[-6:]

    def use(s, slot, j):
        acc[cols_ref[s]] += lax.dot_general(
            buf[slot, j],
            grads[pl.ds(pl.multiple_of(land_ref[s] * BS, BS), BS)],
            (((0,), (0,)), ((), ())),
            preferred_element_type=jnp.float32,
        )

    copies = []
    for i, (ref, start, at, size) in enumerate(piece_plan(piece_refs)):
        copies.append(
            pltpu.make_async_copy(
                ref.at[pl.ds(start, size)], grads.at[pl.ds(at, size)], sems.at[BUFFERS + i]
            )
        )
    for one in copies:
        one.start()
    run = stream_tiles(count_ref[0], tiles_ref, buf, sems, use)
    acc[...] = jnp.zeros_like(acc)
    for one in copies:
        one.wait()
    run()
    out_ref[...] = acc[...].astype(jnp.bfloat16)


def backward_products(land, cols, count, near, far, cores, tiles):
    pieces = near + far + cores
    smem = pl.BlockSpec(memory_space=pltpu.SMEM)
    vmem = pl.BlockSpec(memory_space=pltpu.VMEM)
    hbm = pl.BlockSpec(memory_space=pl.ANY)
    return pl.pallas_call(
        backward_kernel,
        out_shape=jax.ShapeDtypeStruct((32, BS, BS), jnp.bfloat16),
        in_specs=[smem, smem, smem] + [hbm] * (len(pieces) + 1),
        out_specs=vmem,
        scratch_shapes=[
            pltpu.VMEM((32, BS, BS), jnp.float32),
            pltpu.VMEM((BUFFERS, GROUP, BS, BS), jnp.bfloat16),
            pltpu.VMEM((128 * BS, BS), jnp.bfloat16),
            pltpu.SemaphoreType.DMA((BUFFERS + 18,)),
        ],
        compiler_params=pltpu.CompilerParams(vmem_limit_bytes=40 << 20),
        cost_estimate=pl.CostEstimate(
            flops=384 * 2 * BS**3, bytes_accessed=18 << 20, transcendentals=0
        ),
        name="backward_products",
    )(land, cols, count, *pieces, tiles)


def halve(value, side, swap):
    size = value.shape[0] // 2
    mine = lax.dynamic_slice_in_dim(value, side * size, size, 0)
    other = lax.dynamic_slice_in_dim(value, (1 - side) * size, size, 0)
    return mine + send(other, swap)


def tied(*values):
    return lax.optimization_barrier(values)


def forward_slot(j, rel_c, rel_x):
    mine = ((j >= 1) & (j <= 3)) | (((j == 0) | (j == 4)) & (rel_c == 0))
    j = jnp.where(mine, j, (NZ - j) % NZ)
    rel_c = jnp.where(mine, rel_c, 1 - rel_c)
    block = jnp.where(j == 4, 0, jnp.where(j == 0, 7, 7 - 2 * j + rel_c))
    return jnp.where(mine, 0, 16) + rel_x * 8 + block


def backward_slot(j, rel_c, rel_x):
    block = jnp.where(j < 4, 2 * j + rel_c, 9 + 2 * (7 - j) + 1 - rel_c)
    block = jnp.where(j == 4, jnp.where(rel_c == 0, 8, 15), block)
    return rel_x * 16 + block


def total_of(*terms):
    total = terms[0].astype(jnp.float32)
    for term in terms[1:]:
        total = total + term.astype(jnp.float32)
    return total.astype(jnp.bfloat16)


def add_pair(a, b):
    return (a.astype(jnp.float32) + b.astype(jnp.float32)).astype(jnp.bfloat16)


def dense(summed, scale, features, weight, cotangent):
    aggregated = (summed + scale * features.astype(jnp.float32)).astype(jnp.bfloat16)
    pre_act = jnp.dot(aggregated, weight, preferred_element_type=jnp.float32)
    sigma = jax.nn.sigmoid(pre_act)
    activated = (pre_act * sigma).astype(jnp.bfloat16)
    slope = (
        cotangent.astype(jnp.float32) * (sigma * (1.0 + pre_act * (1.0 - sigma)))
    ).astype(jnp.bfloat16)
    weight_part = lax.dot_general(
        aggregated, slope, (((0,), (0,)), ((), ())), preferred_element_type=jnp.float32
    )
    row_grad = lax.dot_general(
        slope, weight, (((1,), (1,)), ((), ())), preferred_element_type=jnp.float32
    ).astype(jnp.bfloat16)
    return activated, weight_part, row_grad


def on_device(
    features, weight, cotangent, self_weight, block_rows, block_cols, block_counts, block_values
):
    tiles = block_values[0, 0]
    rows = block_rows[0, 0]
    cols = block_cols[0, 0]
    count = block_counts[0]
    z = lax.axis_index("z")
    xh = lax.axis_index("xh")
    c = lax.axis_index("c")
    panel_at = rows // 4
    row_z, row_x, row_c = panel_at // 4, (panel_at // 2) % 2, panel_at % 2
    rel_c, rel_x = row_c ^ c, row_x ^ xh
    ahead, behind = (row_z - z) % NZ, (z - row_z) % NZ
    land_fwd = forward_slot(jnp.where(c == 0, ahead, behind), rel_c, rel_x) * 4 + rows % 4
    land_bwd = backward_slot(jnp.where(c == 0, behind, ahead), rel_c, rel_x) * 4 + rows % 4

    panel = lax.all_to_all(jnp.broadcast_to(features, (8, 512, BS)), REP, 0, 0)
    keep, away_far, away_near = forward_products(
        land_fwd, cols, count, panel.reshape(32, BS, BS), tiles
    )
    far = add_pair(keep[32:], send(away_far, CORE_SWAP)).reshape(8, 512, BS)
    away_near, far = tied(away_near, far)
    far_sum = send(far[0], Z_RING)
    near = add_pair(keep[:32], send(away_near, CORE_SWAP)).reshape(8, 512, BS)
    near_sum = send(near[0], Z_RING)
    far_sum = jnp.stack([add_pair(far[1], far_sum), far[2]])
    near_sum = jnp.stack([add_pair(near[1], near_sum), near[2]])
    for at in (3, 5):
        far_sum = add_pair(far[at : at + 2], send(far_sum, Z_RING))
        near_sum = add_pair(near[at : at + 2], send(near_sum, Z_RING))
    far_sum = send(far_sum, Z_RING)
    near_sum = send(near_sum, Z_RING)
    far_sum = total_of(far[7], far_sum[0], send(far_sum[1], CORE_SWAP))
    far_sum = send(far_sum, X_SWAP)
    near_side = send(near_sum[1], CORE_SWAP)
    total = (
        (near[7].astype(jnp.float32) + near_sum[0].astype(jnp.float32))
        + (near_side.astype(jnp.float32) + far_sum.astype(jnp.float32))
    )

    scale = self_weight[0][:, None]
    activated, weight_sum, row_grad = dense(total, scale, features[0], weight, cotangent[0])
    row_grad, weight_sum = tied(row_grad, weight_sum * (1.0 / math.sqrt(32 * 8 * 512)))
    y = lax.axis_index("y")
    sides = (lax.axis_index("xl"), y // 2, y % 2)

    near = jnp.concatenate([row_grad, send(row_grad, CORE_SWAP)], 0)
    x_own = send(row_grad, X_SWAP)
    weight_sum = weight_sum + send(weight_sum, CORE_SWAP)
    x_weight = send(weight_sum, X_SWAP)
    near_ring = [near]
    near_ring.append(send(near, Z_RING))
    x_own, x_weight = tied(x_own, x_weight)
    weight_sum = weight_sum + x_weight
    far = jnp.concatenate([x_own, send(x_own, CORE_SWAP)], 0)
    far_ring = [far]
    far_ring.append(send(far, Z_RING))
    cores = []
    for hop in (2, 3, 4):
        size = 1024 if hop < 4 else 512
        cores.append(send(jnp.concatenate([near_ring[-1], far_ring[-1]], 0), CORE_SWAP))
        near_ring.append(send(near_ring[-1][:size], Z_RING))
        weight_sum = halve(weight_sum, sides[hop - 2], REP_SWAPS[hop - 2])
        near_ring[-1], weight_sum = tied(near_ring[-1], weight_sum)
        far_ring.append(send(far_ring[-1][:size], Z_RING))
    cores.append(send(jnp.concatenate([near_ring[-1], far_ring[-1]], 0), CORE_SWAP))
    columns = backward_products(land_bwd, cols, count, near_ring, far_ring, cores, tiles)
    columns, weight_sum = tied(columns, weight_sum)
    parts = lax.all_to_all(columns.reshape(8, 512, BS), REP, 0, 0)
    for k in (1, 2, 4):
        weight_sum = weight_sum + send(weight_sum, z_flip(k))
    feature_grad = (
        jnp.sum(parts.astype(jnp.float32), 0) + scale * row_grad.astype(jnp.float32)
    ).astype(jnp.bfloat16)[None]
    return activated[None], feature_grad, weight_sum


def solution(mesh):
    fine = Mesh(mesh.devices.reshape(SIZES), AXES)
    placed = (
        P(BLK, REP, None),
        P(),
        P(BLK, REP, None),
        P(BLK, REP),
        P(REP, BLK, None),
        P(REP, BLK, None),
        P(REP, BLK),
        P(REP, BLK, None, None, None),
    )
    return jax.shard_map(
        on_device,
        mesh=fine,
        in_specs=placed,
        out_specs=(P(BLK, REP, None), P(BLK, REP, None), P(REP, None)),
        check_vma=False,
    )
```

```python
import math

import jax
import jax.numpy as jnp
from jax import lax
from jax.experimental import pallas as pl
from jax.experimental.pallas import tpu as pltpu
from jax.sharding import Mesh
from jax.sharding import PartitionSpec as P

AXES = ("xl", "y", "z", "xh", "c")
SIZES = (2, 4, 8, 2, 2)
REP = ("xl", "y")
BLK = ("z", "xh", "c")
NZ = 8
BS = 128
GROUP = 32
BUFFERS = 4


def _pairs(move):
    pairs = []
    for xl in range(2):
        for y in range(4):
            for z in range(8):
                for xh in range(2):
                    for c in range(2):
                        src = (xl, y, z, xh, c)
                        flat = []
                        for at in (src, move(*src)):
                            index = 0
                            for size, value in zip(SIZES, at):
                                index = index * size + value
                            flat.append(index)
                        pairs.append(tuple(flat))
    return pairs


def z_flip(k):
    return _pairs(lambda xl, y, z, xh, c: (xl, y, z ^ k, xh, c))


Z_RING = _pairs(lambda xl, y, z, xh, c: (xl, y, (z + 1 - 2 * c) % 8, xh, c))
REP_SWAPS = (
    _pairs(lambda xl, y, z, xh, c: (1 - xl, y, z, xh, c)),
    _pairs(lambda xl, y, z, xh, c: (xl, y ^ 2, z, xh, c)),
    _pairs(lambda xl, y, z, xh, c: (xl, y ^ 1, z, xh, c)),
)
CORE_SWAP = _pairs(lambda xl, y, z, xh, c: (xl, y, z, xh, 1 - c))
X_SWAP = _pairs(lambda xl, y, z, xh, c: (xl, y, z, 1 - xh, c))


def send(value, pairs):
    return lax.ppermute(value, AXES, pairs)


def stream_tiles(count, tiles_ref, buf, sems, use):
    groups = (count + GROUP - 1) // GROUP

    def copy(group, slot):
        return pltpu.make_async_copy(
            tiles_ref.at[pl.ds(group * GROUP, GROUP)], buf.at[slot], sems.at[slot]
        )

    for first in range(BUFFERS - 1):

        @pl.when(first < groups)
        def _():
            copy(first, first).start()

    def one_group(group, carry):
        slot = lax.rem(group, BUFFERS)
        copy(group, slot).wait()

        @pl.when(group + BUFFERS - 1 < groups)
        def _():
            copy(group + BUFFERS - 1, lax.rem(group + BUFFERS - 1, BUFFERS)).start()

        for j in range(GROUP):
            use(group * GROUP + j, slot, j)
        return carry

    return lambda: lax.fori_loop(0, groups, one_group, 0)


def spread_kernel(one_ref, all_ref, sems):
    copies = [
        pltpu.make_async_copy(one_ref, all_ref.at[i], sems.at[i]) for i in range(all_ref.shape[0])
    ]
    for one in copies:
        one.start()
    for one in copies:
        one.wait()


def spread(value, count):
    return pl.pallas_call(
        spread_kernel,
        out_shape=jax.ShapeDtypeStruct((count,) + value.shape, value.dtype),
        in_specs=[pl.BlockSpec(memory_space=pltpu.VMEM)],
        out_specs=pl.BlockSpec(memory_space=pl.ANY),
        scratch_shapes=[pltpu.SemaphoreType.DMA((count,))],
        name="spread",
    )(value)


def forward_kernel(
    land_ref, cols_ref, count_ref, panel_ref, tiles_ref, keep_ref, away_far_ref, away_near_ref, acc, buf, sems
):
    def use(s, slot, j):
        acc[land_ref[s]] += jnp.dot(
            buf[slot, j], panel_ref[cols_ref[s]], preferred_element_type=jnp.float32
        )

    run = stream_tiles(count_ref[0], tiles_ref, buf, sems, use)
    acc[...] = jnp.zeros_like(acc)
    run()
    away_far_ref[...] = acc[96:].astype(jnp.bfloat16)
    away_near_ref[...] = acc[64:96].astype(jnp.bfloat16)
    keep_ref[...] = acc[:64].astype(jnp.bfloat16)


def forward_products(land, cols, count, panel, tiles):
    smem = pl.BlockSpec(memory_space=pltpu.SMEM)
    vmem = pl.BlockSpec(memory_space=pltpu.VMEM)
    kept = jax.ShapeDtypeStruct((64, BS, BS), jnp.bfloat16)
    away = jax.ShapeDtypeStruct((32, BS, BS), jnp.bfloat16)
    return pl.pallas_call(
        forward_kernel,
        out_shape=(kept, away, away),
        in_specs=[smem, smem, smem, vmem, pl.BlockSpec(memory_space=pl.ANY)],
        out_specs=(vmem, vmem, vmem),
        scratch_shapes=[
            pltpu.VMEM((128, BS, BS), jnp.float32),
            pltpu.VMEM((BUFFERS, GROUP, BS, BS), jnp.bfloat16),
            pltpu.SemaphoreType.DMA((BUFFERS,)),
        ],
        compiler_params=pltpu.CompilerParams(vmem_limit_bytes=40 << 20),
        cost_estimate=pl.CostEstimate(
            flops=384 * 2 * BS**3, bytes_accessed=18 << 20, transcendentals=0
        ),
        name="forward_products",
    )(land, cols, count, panel, tiles)


def piece_plan(refs):
    near, far, cores = refs[:5], refs[5:10], refs[10:]
    plan = []
    at = 0
    for side, ring in enumerate((near, far)):
        for ref in ring:
            plan.append((ref, 0, at, ref.shape[0]))
            at += ref.shape[0]
        for ref in cores:
            size = ref.shape[0] // 2
            plan.append((ref, side * size, at, size))
            at += size
    return plan


def backward_kernel(land_ref, cols_ref, count_ref, *refs):
    piece_refs = refs[:-6]
    tiles_ref, out_ref, acc, buf, grads, sems = refs[-6:]

    def use(s, slot, j):
        acc[cols_ref[s]] += lax.dot_general(
            buf[slot, j],
            grads[pl.ds(pl.multiple_of(land_ref[s] * BS, BS), BS)],
            (((0,), (0,)), ((), ())),
            preferred_element_type=jnp.float32,
        )

    copies = []
    for i, (ref, start, at, size) in enumerate(piece_plan(piece_refs)):
        copies.append(
            pltpu.make_async_copy(
                ref.at[pl.ds(start, size)], grads.at[pl.ds(at, size)], sems.at[BUFFERS + i]
            )
        )
    for one in copies:
        one.start()
    run = stream_tiles(count_ref[0], tiles_ref, buf, sems, use)
    acc[...] = jnp.zeros_like(acc)
    for one in copies:
        one.wait()
    run()
    out_ref[...] = acc[...].astype(jnp.bfloat16)


def backward_products(land, cols, count, near, far, cores, tiles):
    pieces = near + far + cores
    smem = pl.BlockSpec(memory_space=pltpu.SMEM)
    vmem = pl.BlockSpec(memory_space=pltpu.VMEM)
    hbm = pl.BlockSpec(memory_space=pl.ANY)
    return pl.pallas_call(
        backward_kernel,
        out_shape=jax.ShapeDtypeStruct((32, BS, BS), jnp.bfloat16),
        in_specs=[smem, smem, smem] + [hbm] * (len(pieces) + 1),
        out_specs=vmem,
        scratch_shapes=[
            pltpu.VMEM((32, BS, BS), jnp.float32),
            pltpu.VMEM((BUFFERS, GROUP, BS, BS), jnp.bfloat16),
            pltpu.VMEM((128 * BS, BS), jnp.bfloat16),
            pltpu.SemaphoreType.DMA((BUFFERS + 18,)),
        ],
        compiler_params=pltpu.CompilerParams(vmem_limit_bytes=40 << 20),
        cost_estimate=pl.CostEstimate(
            flops=384 * 2 * BS**3, bytes_accessed=18 << 20, transcendentals=0
        ),
        name="backward_products",
    )(land, cols, count, *pieces, tiles)


def halve(value, side, swap):
    size = value.shape[0] // 2
    mine = lax.dynamic_slice_in_dim(value, side * size, size, 0)
    other = lax.dynamic_slice_in_dim(value, (1 - side) * size, size, 0)
    return mine + send(other, swap)


def tied(*values):
    return lax.optimization_barrier(values)


def forward_slot(j, rel_c, rel_x):
    mine = ((j >= 1) & (j <= 3)) | (((j == 0) | (j == 4)) & (rel_c == 0))
    j = jnp.where(mine, j, (NZ - j) % NZ)
    rel_c = jnp.where(mine, rel_c, 1 - rel_c)
    block = jnp.where(j == 4, 0, jnp.where(j == 0, 7, 7 - 2 * j + rel_c))
    return jnp.where(mine, 0, 16) + rel_x * 8 + block


def backward_slot(j, rel_c, rel_x):
    block = jnp.where(j < 4, 2 * j + rel_c, 9 + 2 * (7 - j) + 1 - rel_c)
    block = jnp.where(j == 4, jnp.where(rel_c == 0, 8, 15), block)
    return rel_x * 16 + block


def total_of(*terms):
    total = terms[0].astype(jnp.float32)
    for term in terms[1:]:
        total = total + term.astype(jnp.float32)
    return total.astype(jnp.bfloat16)


def add_pair(a, b):
    return (a.astype(jnp.float32) + b.astype(jnp.float32)).astype(jnp.bfloat16)


def dense(summed, scale, features, weight, cotangent):
    aggregated = (summed + scale * features.astype(jnp.float32)).astype(jnp.bfloat16)
    pre_act = jnp.dot(aggregated, weight, preferred_element_type=jnp.float32)
    sigma = jax.nn.sigmoid(pre_act)
    activated = (pre_act * sigma).astype(jnp.bfloat16)
    slope = (
        cotangent.astype(jnp.float32) * (sigma * (1.0 + pre_act * (1.0 - sigma)))
    ).astype(jnp.bfloat16)
    weight_part = lax.dot_general(
        aggregated, slope, (((0,), (0,)), ((), ())), preferred_element_type=jnp.float32
    )
    row_grad = lax.dot_general(
        slope, weight, (((1,), (1,)), ((), ())), preferred_element_type=jnp.float32
    ).astype(jnp.bfloat16)
    return activated, weight_part, row_grad


def on_device(
    features, weight, cotangent, self_weight, block_rows, block_cols, block_counts, block_values
):
    tiles = block_values[0, 0]
    rows = block_rows[0, 0]
    cols = block_cols[0, 0]
    count = block_counts[0]
    z = lax.axis_index("z")
    xh = lax.axis_index("xh")
    c = lax.axis_index("c")
    panel_at = rows // 4
    row_z, row_x, row_c = panel_at // 4, (panel_at // 2) % 2, panel_at % 2
    rel_c, rel_x = row_c ^ c, row_x ^ xh
    ahead, behind = (row_z - z) % NZ, (z - row_z) % NZ
    land_fwd = forward_slot(jnp.where(c == 0, ahead, behind), rel_c, rel_x) * 4 + rows % 4
    land_bwd = backward_slot(jnp.where(c == 0, behind, ahead), rel_c, rel_x) * 4 + rows % 4

    panel = lax.all_to_all(spread(features[0], 8), REP, 0, 0)
    keep, away_far, away_near = forward_products(
        land_fwd, cols, count, panel.reshape(32, BS, BS), tiles
    )
    far = add_pair(keep[32:], send(away_far, CORE_SWAP)).reshape(8, 512, BS)
    away_near, far = tied(away_near, far)
    far_sum = send(far[0], Z_RING)
    near = add_pair(keep[:32], send(away_near, CORE_SWAP)).reshape(8, 512, BS)
    near_sum = send(near[0], Z_RING)
    far_sum = jnp.stack([add_pair(far[1], far_sum), far[2]])
    near_sum = jnp.stack([add_pair(near[1], near_sum), near[2]])
    for at in (3, 5):
        far_sum = add_pair(far[at : at + 2], send(far_sum, Z_RING))
        near_sum = add_pair(near[at : at + 2], send(near_sum, Z_RING))
    far_sum = send(far_sum, Z_RING)
    near_sum = send(near_sum, Z_RING)
    far_sum = total_of(far[7], far_sum[0], send(far_sum[1], CORE_SWAP))
    far_sum = send(far_sum, X_SWAP)
    near_side = send(near_sum[1], CORE_SWAP)
    total = (
        (near[7].astype(jnp.float32) + near_sum[0].astype(jnp.float32))
        + (near_side.astype(jnp.float32) + far_sum.astype(jnp.float32))
    )

    scale = self_weight[0][:, None]
    activated, weight_sum, row_grad = dense(total, scale, features[0], weight, cotangent[0])
    row_grad, weight_sum = tied(row_grad, weight_sum * (1.0 / math.sqrt(32 * 8 * 512)))
    y = lax.axis_index("y")
    sides = (lax.axis_index("xl"), y // 2, y % 2)

    near = jnp.concatenate([row_grad, send(row_grad, CORE_SWAP)], 0)
    x_own = send(row_grad, X_SWAP)
    weight_sum = weight_sum + send(weight_sum, CORE_SWAP)
    near_ring = [near, send(near, Z_RING)]
    weight_sum = halve(weight_sum, sides[0], REP_SWAPS[0])
    near_ring[-1], weight_sum = tied(near_ring[-1], weight_sum)
    far = jnp.concatenate([x_own, send(x_own, CORE_SWAP)], 0)
    far_ring = [far, send(far, Z_RING)]
    cores = []
    for hop in (2, 3, 4):
        size = 1024 if hop < 4 else 512
        cores.append(send(jnp.concatenate([near_ring[-1], far_ring[-1]], 0), CORE_SWAP))
        near_ring.append(send(near_ring[-1][:size], Z_RING))
        if hop < 4:
            weight_sum = halve(weight_sum, sides[hop - 1], REP_SWAPS[hop - 1])
        else:
            weight_sum = weight_sum + send(weight_sum, X_SWAP)
        near_ring[-1], weight_sum = tied(near_ring[-1], weight_sum)
        far_ring.append(send(far_ring[-1][:size], Z_RING))
    cores.append(send(jnp.concatenate([near_ring[-1], far_ring[-1]], 0), CORE_SWAP))
    columns = backward_products(land_bwd, cols, count, near_ring, far_ring, cores, tiles)
    columns, weight_sum = tied(columns, weight_sum)
    parts = lax.all_to_all(columns.reshape(8, 512, BS), REP, 0, 0)
    for k in (1, 3, 7):
        weight_sum = weight_sum + send(weight_sum, z_flip(k))
    feature_grad = (
        jnp.sum(parts.astype(jnp.float32), 0) + scale * row_grad.astype(jnp.float32)
    ).astype(jnp.bfloat16)[None]
    return activated[None], feature_grad, weight_sum


def solution(mesh):
    fine = Mesh(mesh.devices.reshape(SIZES), AXES)
    placed = (
        P(BLK, REP, None),
        P(),
        P(BLK, REP, None),
        P(BLK, REP),
        P(REP, BLK, None),
        P(REP, BLK, None),
        P(REP, BLK),
        P(REP, BLK, None, None, None),
    )
    return jax.shard_map(
        on_device,
        mesh=fine,
        in_specs=placed,
        out_specs=(P(BLK, REP, None), P(BLK, REP, None), P(REP, None)),
        check_vma=False,
    )
```

```python
import math

import jax
import jax.numpy as jnp
from jax import lax
from jax.experimental import pallas as pl
from jax.experimental.pallas import tpu as pltpu
from jax.sharding import Mesh
from jax.sharding import PartitionSpec as P

AXES = ("xl", "y", "z", "xh", "c")
SIZES = (2, 4, 8, 2, 2)
REP = ("xl", "y")
BLK = ("z", "xh", "c")
NZ = 8
BS = 128
GROUP = 64
BUFFERS = 3


def _pairs(move):
    pairs = []
    for xl in range(2):
        for y in range(4):
            for z in range(8):
                for xh in range(2):
                    for c in range(2):
                        src = (xl, y, z, xh, c)
                        flat = []
                        for at in (src, move(*src)):
                            index = 0
                            for size, value in zip(SIZES, at):
                                index = index * size + value
                            flat.append(index)
                        pairs.append(tuple(flat))
    return pairs


def z_flip(k):
    return _pairs(lambda xl, y, z, xh, c: (xl, y, z ^ k, xh, c))


Z_RING = _pairs(lambda xl, y, z, xh, c: (xl, y, (z + 1 - 2 * c) % 8, xh, c))
REP_SWAPS = (
    _pairs(lambda xl, y, z, xh, c: (1 - xl, y, z, xh, c)),
    _pairs(lambda xl, y, z, xh, c: (xl, y ^ 2, z, xh, c)),
    _pairs(lambda xl, y, z, xh, c: (xl, y ^ 1, z, xh, c)),
)
CORE_SWAP = _pairs(lambda xl, y, z, xh, c: (xl, y, z, xh, 1 - c))
X_SWAP = _pairs(lambda xl, y, z, xh, c: (xl, y, z, 1 - xh, c))


def send(value, pairs):
    return lax.ppermute(value, AXES, pairs)


def stream_tiles(count, tiles_ref, buf, sems, use):
    groups = (count + GROUP - 1) // GROUP

    def copy(group, slot):
        return pltpu.make_async_copy(
            tiles_ref.at[pl.ds(group * GROUP, GROUP)], buf.at[slot], sems.at[slot]
        )

    for first in range(BUFFERS - 1):

        @pl.when(first < groups)
        def _():
            copy(first, first).start()

    def one_group(group, carry):
        slot = lax.rem(group, BUFFERS)
        copy(group, slot).wait()

        @pl.when(group + BUFFERS - 1 < groups)
        def _():
            copy(group + BUFFERS - 1, lax.rem(group + BUFFERS - 1, BUFFERS)).start()

        for j in range(GROUP):
            use(group * GROUP + j, slot, j)
        return carry

    return lambda: lax.fori_loop(0, groups, one_group, 0)


def spread_kernel(one_ref, all_ref, sems):
    copies = [
        pltpu.make_async_copy(one_ref, all_ref.at[i], sems.at[i]) for i in range(all_ref.shape[0])
    ]
    for one in copies:
        one.start()
    for one in copies:
        one.wait()


def spread(value, count):
    return pl.pallas_call(
        spread_kernel,
        out_shape=jax.ShapeDtypeStruct((count,) + value.shape, value.dtype),
        in_specs=[pl.BlockSpec(memory_space=pltpu.VMEM)],
        out_specs=pl.BlockSpec(memory_space=pl.ANY),
        scratch_shapes=[pltpu.SemaphoreType.DMA((count,))],
        name="spread",
    )(value)


def forward_kernel(
    land_ref, cols_ref, count_ref, panel_ref, tiles_ref, keep_ref, away_far_ref, away_near_ref, acc, buf, sems
):
    def use(s, slot, j):
        acc[land_ref[s]] += jnp.dot(
            buf[slot, j], panel_ref[cols_ref[s]], preferred_element_type=jnp.float32
        )

    run = stream_tiles(count_ref[0], tiles_ref, buf, sems, use)
    acc[...] = jnp.zeros_like(acc)
    run()
    away_far_ref[...] = acc[96:].astype(jnp.bfloat16)
    away_near_ref[...] = acc[64:96].astype(jnp.bfloat16)
    keep_ref[...] = acc[:64].astype(jnp.bfloat16)


def forward_products(land, cols, count, panel, tiles):
    smem = pl.BlockSpec(memory_space=pltpu.SMEM)
    vmem = pl.BlockSpec(memory_space=pltpu.VMEM)
    kept = jax.ShapeDtypeStruct((64, BS, BS), jnp.bfloat16)
    away = jax.ShapeDtypeStruct((32, BS, BS), jnp.bfloat16)
    return pl.pallas_call(
        forward_kernel,
        out_shape=(kept, away, away),
        in_specs=[smem, smem, smem, vmem, pl.BlockSpec(memory_space=pl.ANY)],
        out_specs=(vmem, vmem, vmem),
        scratch_shapes=[
            pltpu.VMEM((128, BS, BS), jnp.float32),
            pltpu.VMEM((BUFFERS, GROUP, BS, BS), jnp.bfloat16),
            pltpu.SemaphoreType.DMA((BUFFERS,)),
        ],
        compiler_params=pltpu.CompilerParams(vmem_limit_bytes=40 << 20),
        cost_estimate=pl.CostEstimate(
            flops=384 * 2 * BS**3, bytes_accessed=18 << 20, transcendentals=0
        ),
        name="forward_products",
    )(land, cols, count, panel, tiles)


def backward_kernel(
    land_ref, cols_ref, count_ref, grads_ref, tiles_ref, out_ref, acc, buf, sems
):
    def use(s, slot, j):
        acc[cols_ref[s]] += lax.dot_general(
            buf[slot, j],
            grads_ref[land_ref[s]],
            (((0,), (0,)), ((), ())),
            preferred_element_type=jnp.float32,
        )

    run = stream_tiles(count_ref[0], tiles_ref, buf, sems, use)
    acc[...] = jnp.zeros_like(acc)
    run()
    out_ref[...] = acc[...].astype(jnp.bfloat16)


def backward_products(land, cols, count, grads, tiles):
    smem = pl.BlockSpec(memory_space=pltpu.SMEM)
    vmem = pl.BlockSpec(memory_space=pltpu.VMEM)
    return pl.pallas_call(
        backward_kernel,
        out_shape=jax.ShapeDtypeStruct((32, BS, BS), jnp.bfloat16),
        in_specs=[smem, smem, smem, vmem, pl.BlockSpec(memory_space=pl.ANY)],
        out_specs=vmem,
        scratch_shapes=[
            pltpu.VMEM((32, BS, BS), jnp.float32),
            pltpu.VMEM((BUFFERS, GROUP, BS, BS), jnp.bfloat16),
            pltpu.SemaphoreType.DMA((BUFFERS,)),
        ],
        compiler_params=pltpu.CompilerParams(vmem_limit_bytes=44 << 20),
        cost_estimate=pl.CostEstimate(
            flops=384 * 2 * BS**3, bytes_accessed=18 << 20, transcendentals=0
        ),
        name="backward_products",
    )(land, cols, count, grads, tiles)


def halve(value, side, swap):
    size = value.shape[0] // 2
    mine = lax.dynamic_slice_in_dim(value, side * size, size, 0)
    other = lax.dynamic_slice_in_dim(value, (1 - side) * size, size, 0)
    return mine + send(other, swap)


def tied(*values):
    return lax.optimization_barrier(values)


def forward_slot(j, rel_c, rel_x):
    mine = ((j >= 1) & (j <= 3)) | (((j == 0) | (j == 4)) & (rel_c == 0))
    j = jnp.where(mine, j, (NZ - j) % NZ)
    rel_c = jnp.where(mine, rel_c, 1 - rel_c)
    block = jnp.where(j == 4, 0, jnp.where(j == 0, 7, 7 - 2 * j + rel_c))
    return jnp.where(mine, 0, 16) + rel_x * 8 + block


def backward_slot(j, rel_c, rel_x):
    block = jnp.where(j < 4, 2 * j + rel_c, 9 + 2 * (7 - j) + 1 - rel_c)
    block = jnp.where(j == 4, jnp.where(rel_c == 0, 8, 15), block)
    return rel_x * 16 + block


def total_of(*terms):
    total = terms[0].astype(jnp.float32)
    for term in terms[1:]:
        total = total + term.astype(jnp.float32)
    return total.astype(jnp.bfloat16)


def add_pair(a, b):
    return (a.astype(jnp.float32) + b.astype(jnp.float32)).astype(jnp.bfloat16)


def dense(summed, scale, features, weight, cotangent):
    aggregated = (summed + scale * features.astype(jnp.float32)).astype(jnp.bfloat16)
    pre_act = jnp.dot(aggregated, weight, preferred_element_type=jnp.float32)
    sigma = jax.nn.sigmoid(pre_act)
    activated = (pre_act * sigma).astype(jnp.bfloat16)
    slope = (
        cotangent.astype(jnp.float32) * (sigma * (1.0 + pre_act * (1.0 - sigma)))
    ).astype(jnp.bfloat16)
    weight_part = lax.dot_general(
        aggregated, slope, (((0,), (0,)), ((), ())), preferred_element_type=jnp.float32
    )
    row_grad = lax.dot_general(
        slope, weight, (((1,), (1,)), ((), ())), preferred_element_type=jnp.float32
    ).astype(jnp.bfloat16)
    return activated, weight_part, row_grad


def on_device(
    features, weight, cotangent, self_weight, block_rows, block_cols, block_counts, block_values
):
    tiles = block_values[0, 0]
    rows = block_rows[0, 0]
    cols = block_cols[0, 0]
    count = block_counts[0]
    z = lax.axis_index("z")
    xh = lax.axis_index("xh")
    c = lax.axis_index("c")
    panel_at = rows // 4
    row_z, row_x, row_c = panel_at // 4, (panel_at // 2) % 2, panel_at % 2
    rel_c, rel_x = row_c ^ c, row_x ^ xh
    ahead, behind = (row_z - z) % NZ, (z - row_z) % NZ
    land_fwd = forward_slot(jnp.where(c == 0, ahead, behind), rel_c, rel_x) * 4 + rows % 4
    land_bwd = backward_slot(jnp.where(c == 0, behind, ahead), rel_c, rel_x) * 4 + rows % 4

    panel = lax.all_to_all(spread(features[0], 8), REP, 0, 0)
    keep, away_far, away_near = forward_products(
        land_fwd, cols, count, panel.reshape(32, BS, BS), tiles
    )
    far = add_pair(keep[32:], send(away_far, CORE_SWAP)).reshape(8, 512, BS)
    away_near, far = tied(away_near, far)
    far_sum = send(far[0], Z_RING)
    near = add_pair(keep[:32], send(away_near, CORE_SWAP)).reshape(8, 512, BS)
    near_sum = send(near[0], Z_RING)
    far_sum = jnp.stack([add_pair(far[1], far_sum), far[2]])
    near_sum = jnp.stack([add_pair(near[1], near_sum), near[2]])
    for at in (3, 5):
        far_sum = add_pair(far[at : at + 2], send(far_sum, Z_RING))
        near_sum = add_pair(near[at : at + 2], send(near_sum, Z_RING))
    far_sum = send(far_sum, Z_RING)
    near_sum = send(near_sum, Z_RING)
    far_sum = total_of(far[7], far_sum[0], send(far_sum[1], CORE_SWAP))
    far_sum = send(far_sum, X_SWAP)
    near_side = send(near_sum[1], CORE_SWAP)
    total = (
        (near[7].astype(jnp.float32) + near_sum[0].astype(jnp.float32))
        + (near_side.astype(jnp.float32) + far_sum.astype(jnp.float32))
    )

    scale = self_weight[0][:, None]
    activated, weight_sum, row_grad = dense(total, scale, features[0], weight, cotangent[0])
    row_grad, weight_sum = tied(row_grad, weight_sum * (1.0 / math.sqrt(32 * 8 * 512)))
    y = lax.axis_index("y")
    sides = (lax.axis_index("xl"), y // 2, y % 2)

    near = jnp.concatenate([row_grad, send(row_grad, CORE_SWAP)], 0)
    x_own = send(row_grad, X_SWAP)
    weight_sum = weight_sum + send(weight_sum, CORE_SWAP)
    near_ring = [near, send(near, Z_RING)]
    weight_sum = halve(weight_sum, sides[0], REP_SWAPS[0])
    near_ring[-1], weight_sum = tied(near_ring[-1], weight_sum)
    far = jnp.concatenate([x_own, send(x_own, CORE_SWAP)], 0)
    far_ring = [far, send(far, Z_RING)]
    cores = []
    for hop in (2, 3, 4):
        size = 1024 if hop < 4 else 512
        cores.append(send(jnp.concatenate([near_ring[-1], far_ring[-1]], 0), CORE_SWAP))
        near_ring.append(send(near_ring[-1][:size], Z_RING))
        if hop < 4:
            weight_sum = halve(weight_sum, sides[hop - 1], REP_SWAPS[hop - 1])
        else:
            weight_sum = weight_sum + send(weight_sum, X_SWAP)
        near_ring[-1], weight_sum = tied(near_ring[-1], weight_sum)
        far_ring.append(send(far_ring[-1][:size], Z_RING))
    cores.append(send(jnp.concatenate([near_ring[-1], far_ring[-1]], 0), CORE_SWAP))
    near_ring, far_ring, cores = tied(near_ring, far_ring, cores)
    halves = [jnp.split(core, 2) for core in cores]
    grads = near_ring + [half[0] for half in halves]
    grads += far_ring + [half[1] for half in halves]
    grads = jnp.concatenate(grads, 0).reshape(128, BS, BS)
    columns = backward_products(land_bwd, cols, count, grads, tiles)
    columns, weight_sum = tied(columns, weight_sum)
    parts = lax.all_to_all(columns.reshape(8, 512, BS), REP, 0, 0)
    for k in (1, 3, 7):
        weight_sum = weight_sum + send(weight_sum, z_flip(k))
    feature_grad = (
        jnp.sum(parts.astype(jnp.float32), 0) + scale * row_grad.astype(jnp.float32)
    ).astype(jnp.bfloat16)[None]
    return activated[None], feature_grad, weight_sum


def solution(mesh):
    fine = Mesh(mesh.devices.reshape(SIZES), AXES)
    placed = (
        P(BLK, REP, None),
        P(),
        P(BLK, REP, None),
        P(BLK, REP),
        P(REP, BLK, None),
        P(REP, BLK, None),
        P(REP, BLK),
        P(REP, BLK, None, None, None),
    )
    return jax.shard_map(
        on_device,
        mesh=fine,
        in_specs=placed,
        out_specs=(P(BLK, REP, None), P(BLK, REP, None), P(REP, None)),
        check_vma=False,
    )
```

```python
import math

import jax
import jax.numpy as jnp
from jax import lax
from jax.experimental import pallas as pl
from jax.experimental.pallas import tpu as pltpu
from jax.sharding import Mesh
from jax.sharding import PartitionSpec as P

AXES = ("xl", "y", "z", "xh", "c")
SIZES = (2, 4, 8, 2, 2)
REP = ("xl", "y")
BLK = ("z", "xh", "c")
NZ = 8
BS = 128
GROUP = 64
BUFFERS = 3


def _pairs(move):
    pairs = []
    for xl in range(2):
        for y in range(4):
            for z in range(8):
                for xh in range(2):
                    for c in range(2):
                        src = (xl, y, z, xh, c)
                        flat = []
                        for at in (src, move(*src)):
                            index = 0
                            for size, value in zip(SIZES, at):
                                index = index * size + value
                            flat.append(index)
                        pairs.append(tuple(flat))
    return pairs


def z_flip(k):
    return _pairs(lambda xl, y, z, xh, c: (xl, y, z ^ k, xh, c))


Z_RING = _pairs(lambda xl, y, z, xh, c: (xl, y, (z + 1 - 2 * c) % 8, xh, c))
REP_SWAPS = (
    _pairs(lambda xl, y, z, xh, c: (1 - xl, y, z, xh, c)),
    _pairs(lambda xl, y, z, xh, c: (xl, y ^ 3, z, xh, c)),
    _pairs(lambda xl, y, z, xh, c: (xl, y ^ 1, z, xh, c)),
)
CORE_SWAP = _pairs(lambda xl, y, z, xh, c: (xl, y, z, xh, 1 - c))
X_SWAP = _pairs(lambda xl, y, z, xh, c: (xl, y, z, 1 - xh, c))


def send(value, pairs):
    return lax.ppermute(value, AXES, pairs)


def stream_tiles(count, tiles_ref, buf, sems, use):
    groups = (count + GROUP - 1) // GROUP

    def copy(group, slot):
        return pltpu.make_async_copy(
            tiles_ref.at[pl.ds(group * GROUP, GROUP)], buf.at[slot], sems.at[slot]
        )

    for first in range(BUFFERS - 1):

        @pl.when(first < groups)
        def _():
            copy(first, first).start()

    def one_group(group, carry):
        slot = lax.rem(group, BUFFERS)
        copy(group, slot).wait()

        @pl.when(group + BUFFERS - 1 < groups)
        def _():
            copy(group + BUFFERS - 1, lax.rem(group + BUFFERS - 1, BUFFERS)).start()

        for j in range(GROUP):
            use(group * GROUP + j, slot, j)
        return carry

    return lambda: lax.fori_loop(0, groups, one_group, 0)


def spread_kernel(one_ref, all_ref, sems):
    copies = [
        pltpu.make_async_copy(one_ref, all_ref.at[i], sems.at[i]) for i in range(all_ref.shape[0])
    ]
    for one in copies:
        one.start()
    for one in copies:
        one.wait()


def spread(value, count):
    return pl.pallas_call(
        spread_kernel,
        out_shape=jax.ShapeDtypeStruct((count,) + value.shape, value.dtype),
        in_specs=[pl.BlockSpec(memory_space=pltpu.VMEM)],
        out_specs=pl.BlockSpec(memory_space=pl.ANY),
        scratch_shapes=[pltpu.SemaphoreType.DMA((count,))],
        name="spread",
    )(value)


def forward_kernel(
    land_ref, cols_ref, count_ref, panel_ref, tiles_ref, keep_ref, away_far_ref, away_near_ref, acc, buf, sems
):
    def use(s, slot, j):
        acc[land_ref[s]] += jnp.dot(
            buf[slot, j], panel_ref[cols_ref[s]], preferred_element_type=jnp.float32
        )

    run = stream_tiles(count_ref[0], tiles_ref, buf, sems, use)
    acc[...] = jnp.zeros_like(acc)
    run()
    away_far_ref[...] = acc[96:].astype(jnp.bfloat16)
    away_near_ref[...] = acc[64:96].astype(jnp.bfloat16)
    keep_ref[...] = acc[:64].astype(jnp.bfloat16)


def forward_products(land, cols, count, panel, tiles):
    smem = pl.BlockSpec(memory_space=pltpu.SMEM)
    vmem = pl.BlockSpec(memory_space=pltpu.VMEM)
    kept = jax.ShapeDtypeStruct((64, BS, BS), jnp.bfloat16)
    away = jax.ShapeDtypeStruct((32, BS, BS), jnp.bfloat16)
    return pl.pallas_call(
        forward_kernel,
        out_shape=(kept, away, away),
        in_specs=[smem, smem, smem, vmem, pl.BlockSpec(memory_space=pl.ANY)],
        out_specs=(vmem, vmem, vmem),
        scratch_shapes=[
            pltpu.VMEM((128, BS, BS), jnp.float32),
            pltpu.VMEM((BUFFERS, GROUP, BS, BS), jnp.bfloat16),
            pltpu.SemaphoreType.DMA((BUFFERS,)),
        ],
        compiler_params=pltpu.CompilerParams(vmem_limit_bytes=40 << 20),
        cost_estimate=pl.CostEstimate(
            flops=384 * 2 * BS**3, bytes_accessed=18 << 20, transcendentals=0
        ),
        name="forward_products",
    )(land, cols, count, panel, tiles)


def backward_kernel(
    land_ref, cols_ref, count_ref, grads_ref, tiles_ref, out_ref, acc, buf, sems
):
    def use(s, slot, j):
        acc[cols_ref[s]] += lax.dot_general(
            buf[slot, j],
            grads_ref[land_ref[s]],
            (((0,), (0,)), ((), ())),
            preferred_element_type=jnp.float32,
        )

    run = stream_tiles(count_ref[0], tiles_ref, buf, sems, use)
    acc[...] = jnp.zeros_like(acc)
    run()
    out_ref[...] = acc[...].astype(jnp.bfloat16)


def backward_products(land, cols, count, grads, tiles):
    smem = pl.BlockSpec(memory_space=pltpu.SMEM)
    vmem = pl.BlockSpec(memory_space=pltpu.VMEM)
    return pl.pallas_call(
        backward_kernel,
        out_shape=jax.ShapeDtypeStruct((32, BS, BS), jnp.bfloat16),
        in_specs=[smem, smem, smem, vmem, pl.BlockSpec(memory_space=pl.ANY)],
        out_specs=vmem,
        scratch_shapes=[
            pltpu.VMEM((32, BS, BS), jnp.float32),
            pltpu.VMEM((BUFFERS, GROUP, BS, BS), jnp.bfloat16),
            pltpu.SemaphoreType.DMA((BUFFERS,)),
        ],
        compiler_params=pltpu.CompilerParams(vmem_limit_bytes=44 << 20),
        cost_estimate=pl.CostEstimate(
            flops=384 * 2 * BS**3, bytes_accessed=18 << 20, transcendentals=0
        ),
        name="backward_products",
    )(land, cols, count, grads, tiles)


def halve(value, side, swap):
    size = value.shape[0] // 2
    mine = lax.dynamic_slice_in_dim(value, side * size, size, 0)
    other = lax.dynamic_slice_in_dim(value, (1 - side) * size, size, 0)
    return mine + send(other, swap)


def tied(*values):
    return lax.optimization_barrier(values)


def forward_slot(j, rel_c, rel_x):
    mine = ((j >= 1) & (j <= 3)) | (((j == 0) | (j == 4)) & (rel_c == 0))
    j = jnp.where(mine, j, (NZ - j) % NZ)
    rel_c = jnp.where(mine, rel_c, 1 - rel_c)
    block = jnp.where(j == 4, 0, jnp.where(j == 0, 7, 7 - 2 * j + rel_c))
    return jnp.where(mine, 0, 16) + rel_x * 8 + block


def backward_slot(j, rel_c, rel_x):
    block = jnp.where(j < 4, 2 * j + rel_c, 9 + 2 * (7 - j) + 1 - rel_c)
    block = jnp.where(j == 4, jnp.where(rel_c == 0, 8, 15), block)
    return rel_x * 16 + block


def total_of(*terms):
    total = terms[0].astype(jnp.float32)
    for term in terms[1:]:
        total = total + term.astype(jnp.float32)
    return total.astype(jnp.bfloat16)


def add_pair(a, b):
    return (a.astype(jnp.float32) + b.astype(jnp.float32)).astype(jnp.bfloat16)


def dense(summed, scale, features, weight, cotangent):
    aggregated = (summed + scale * features.astype(jnp.float32)).astype(jnp.bfloat16)
    pre_act = jnp.dot(aggregated, weight, preferred_element_type=jnp.float32)
    sigma = jax.nn.sigmoid(pre_act)
    activated = (pre_act * sigma).astype(jnp.bfloat16)
    slope = (
        cotangent.astype(jnp.float32) * (sigma * (1.0 + pre_act * (1.0 - sigma)))
    ).astype(jnp.bfloat16)
    weight_part = lax.dot_general(
        aggregated, slope, (((0,), (0,)), ((), ())), preferred_element_type=jnp.float32
    )
    row_grad = lax.dot_general(
        slope, weight, (((1,), (1,)), ((), ())), preferred_element_type=jnp.float32
    ).astype(jnp.bfloat16)
    return activated, weight_part, row_grad


def on_device(
    features, weight, cotangent, self_weight, block_rows, block_cols, block_counts, block_values
):
    tiles = block_values[0, 0]
    rows = block_rows[0, 0]
    cols = block_cols[0, 0]
    count = block_counts[0]
    z = lax.axis_index("z")
    xh = lax.axis_index("xh")
    c = lax.axis_index("c")
    panel_at = rows // 4
    row_z, row_x, row_c = panel_at // 4, (panel_at // 2) % 2, panel_at % 2
    rel_c, rel_x = row_c ^ c, row_x ^ xh
    ahead, behind = (row_z - z) % NZ, (z - row_z) % NZ
    land_fwd = forward_slot(jnp.where(c == 0, ahead, behind), rel_c, rel_x) * 4 + rows % 4
    land_bwd = backward_slot(jnp.where(c == 0, behind, ahead), rel_c, rel_x) * 4 + rows % 4

    panel = lax.all_to_all(spread(features[0], 8), REP, 0, 0)
    keep, away_far, away_near = forward_products(
        land_fwd, cols, count, panel.reshape(32, BS, BS), tiles
    )
    far = add_pair(keep[32:], send(away_far, CORE_SWAP)).reshape(8, 512, BS)
    away_near, far = tied(away_near, far)
    far_sum = send(far[0], Z_RING)
    near = add_pair(keep[:32], send(away_near, CORE_SWAP)).reshape(8, 512, BS)
    near_sum = send(near[0], Z_RING)
    far_sum = jnp.stack([add_pair(far[1], far_sum), far[2]])
    near_sum = jnp.stack([add_pair(near[1], near_sum), near[2]])
    for at in (3, 5):
        far_sum = add_pair(far[at : at + 2], send(far_sum, Z_RING))
        near_sum = add_pair(near[at : at + 2], send(near_sum, Z_RING))
    far_sum = send(far_sum, Z_RING)
    near_sum = send(near_sum, Z_RING)
    far_sum = total_of(far[7], far_sum[0], send(far_sum[1], CORE_SWAP))
    far_sum = send(far_sum, X_SWAP)
    near_side = send(near_sum[1], CORE_SWAP)
    total = (
        (near[7].astype(jnp.float32) + near_sum[0].astype(jnp.float32))
        + (near_side.astype(jnp.float32) + far_sum.astype(jnp.float32))
    )

    scale = self_weight[0][:, None]
    activated, weight_sum, row_grad = dense(total, scale, features[0], weight, cotangent[0])
    row_grad, weight_sum = tied(row_grad, weight_sum * (1.0 / math.sqrt(32 * 8 * 512)))
    y = lax.axis_index("y")
    sides = (lax.axis_index("xl"), y // 2, y % 2)

    near = jnp.concatenate([row_grad, send(row_grad, CORE_SWAP)], 0)
    x_own = send(row_grad, X_SWAP)
    weight_sum = weight_sum + send(weight_sum, CORE_SWAP)
    near_ring = [near, send(near, Z_RING)]
    weight_sum = halve(weight_sum, sides[0], REP_SWAPS[0])
    near_ring[-1], weight_sum = tied(near_ring[-1], weight_sum)
    far = jnp.concatenate([x_own, send(x_own, CORE_SWAP)], 0)
    far_ring = [far, send(far, Z_RING)]
    cores = []
    for hop in (2, 3, 4):
        size = 1024 if hop < 4 else 512
        cores.append(send(jnp.concatenate([near_ring[-1], far_ring[-1]], 0), CORE_SWAP))
        near_ring.append(send(near_ring[-1][:size], Z_RING))
        if hop < 4:
            weight_sum = halve(weight_sum, sides[hop - 1], REP_SWAPS[hop - 1])
        else:
            weight_sum = weight_sum + send(weight_sum, X_SWAP)
        near_ring[-1], weight_sum = tied(near_ring[-1], weight_sum)
        far_ring.append(send(far_ring[-1][:size], Z_RING))
    cores.append(send(jnp.concatenate([near_ring[-1], far_ring[-1]], 0), CORE_SWAP))
    near_ring, far_ring, cores = tied(near_ring, far_ring, cores)
    halves = [jnp.split(core, 2) for core in cores]
    grads = near_ring + [half[0] for half in halves]
    grads += far_ring + [half[1] for half in halves]
    grads = jnp.concatenate(grads, 0).reshape(128, BS, BS)
    columns = backward_products(land_bwd, cols, count, grads, tiles)
    columns, weight_sum = tied(columns, weight_sum)
    parts = lax.all_to_all(columns.reshape(8, 512, BS), REP, 0, 0)
    for k in (1, 2, 6):
        weight_sum = weight_sum + send(weight_sum, z_flip(k))
    feature_grad = (
        jnp.sum(parts.astype(jnp.float32), 0) + scale * row_grad.astype(jnp.float32)
    ).astype(jnp.bfloat16)[None]
    return activated[None], feature_grad, weight_sum


def solution(mesh):
    fine = Mesh(mesh.devices.reshape(SIZES), AXES)
    placed = (
        P(BLK, REP, None),
        P(),
        P(BLK, REP, None),
        P(BLK, REP),
        P(REP, BLK, None),
        P(REP, BLK, None),
        P(REP, BLK),
        P(REP, BLK, None, None, None),
    )
    return jax.shard_map(
        on_device,
        mesh=fine,
        in_specs=placed,
        out_specs=(P(BLK, REP, None), P(BLK, REP, None), P(REP, None)),
        check_vma=False,
    )
```
